32 devices in a mesh: groups: 2 (over x), aux: 8 (over z, y), bas: 2 (over core).
Axes of the slice: x: 2, y: 2, z: 4, core: 2. Of those that a mesh axis runs over, the one named last changes fastest.
Arguments:
- factors: bfloat16 [128, 16, 4, 128, 128], P(('groups', 'aux'), 'bas'), parts along dimension 0, may hold values from -6 to 6
- tile_cols: int32 [32, 4], P(('groups', 'bas')), parts along dimension 0, may hold values from 0 to 15, as said below
- tile_live: int32 [32, 4], P(('groups', 'bas')), parts along dimension 0, may hold values from 0 to 1, as said below
- coefficients: bfloat16 [1024, 2048], P('groups'), parts along dimension 0, may hold values from -0.25 to 0.25
- batch_rows: int32 [4, 128], P('groups'), parts along dimension 0, may hold values from 0 to 511, as said below
Outputs:
- exchange: float32 [4096, 2048], P(('groups', 'bas'), 'aux'), parts along dimension 0
The draws below stay inside these ranges and needn't reach their ends.
There are 2 independent parts, one for each index of `groups`. The reference program is written for one: setup_inputs(seed, part) draws one part's arguments, and reference() takes and returns one part's arrays. A program takes and returns all parts, laid end to end along the dimension named above; each array names one. Nothing has to cross between parts.
Inputs may be any that keep to these rules, and one draw needn't show every extreme that they name: `tile_cols`: in each row t the 4 column tiles are distinct and slot 0 holds t itself. `tile_live`: slot 0 of every row is live. `batch_rows`: all 256 entries are distinct.
All inputs are finite; a program needn't handle non-finite values.
Results may differ from the reference program's by a relative error of at most 0.0014.
Values may be sent and summed in bfloat16 or wider, within the bound.
A program may use at most 128 MiB of HBM per device.

```python
import math
import jax
import jax.numpy as jnp
from jax import lax

TILE = 128
TILES = 16
SLOTS = 4
AUX_DEV = 8
OCC = 128
BATCHES = 2
NBAS = 2048
AUX = 64
NORB = 512
N_AUX = 8


def draw_tile_cols(key, part):
    key = jax.random.fold_in(key, 11)
    row_keys = jax.random.split(key, TILES)

    def one_row(row_key):
        return jax.random.permutation(row_key, TILES - 1)[:SLOTS - 1] + 1
    offsets = jax.vmap(one_row)(row_keys)
    offsets = jnp.concatenate([jnp.zeros((TILES, 1), jnp.int32), offsets.astype(jnp.int32)], axis=1)
    row_ids = jnp.arange(TILES, dtype=jnp.int32)[:, None]
    return ((row_ids + offsets) % TILES).astype(jnp.int32)


def draw_tile_live(key, part):
    key = jax.random.fold_in(key, 23)
    coins = jax.random.randint(key, (TILES, SLOTS), 0, 3)
    live_mask = jnp.where(coins < 2, 1, 0).astype(jnp.int32)
    live_mask = live_mask.at[:, 0].set(1)
    live_mask = live_mask.at[0, SLOTS - 1].set(0)
    return live_mask


def draw_batch_rows(key, part):
    key = jax.random.fold_in(key, 37)
    first_key, second_key = jax.random.split(key)
    middle = jax.random.permutation(first_key, NORB - 2)[:BATCHES * OCC - 2] + 1
    chosen = jnp.concatenate([jnp.array([0, NORB - 1], jnp.int32), middle.astype(jnp.int32)])
    chosen = jax.random.permutation(second_key, chosen)
    return chosen.reshape(BATCHES, OCC).astype(jnp.int32)


def block_levels(rng, shape, cuts, smallest, high):
    factor_of, own = 1.0, jax.random.fold_in(rng, 6)
    for dim, parts in cuts:
        draws = jnp.exp(jax.random.uniform(jax.random.fold_in(own, dim), (parts,), jnp.float32, smallest / len(cuts), high / len(cuts)))
        factor_of = factor_of * jnp.repeat(draws, shape[dim] // parts).reshape([-1 if axis == dim else 1 for axis in range(len(shape))])
    return factor_of


def gaussian(stream_key, extent, deviation, limit, pieces=(), held_as=jnp.bfloat16):
    values = jax.random.normal(stream_key, extent, jnp.float32) * deviation
    if len(pieces) > 0:
        values = block_levels(stream_key, extent, pieces, -0.22, 0.18) * values
    return jnp.clip(values, min=-limit, max=limit).astype(held_as)


def setup_inputs(seed: int = 0, part: int = 0) -> dict:
    arg_keys = jax.random.split(jax.random.key(seed), 6)
    own_keys = jax.random.split(jax.random.fold_in(arg_keys[5], part), 6)
    factors = gaussian(own_keys[0], (AUX, TILES, SLOTS, TILE, TILE), 1.0, 6.0, ((0, 8), (1, 2)))
    tile_cols = draw_tile_cols(jax.random.fold_in(jax.random.fold_in(arg_keys[5], part), 71), part)
    tile_live = draw_tile_live(jax.random.fold_in(jax.random.fold_in(arg_keys[5], part), 71), part)
    coefficients = gaussian(own_keys[3], (NORB, NBAS), (SLOTS * TILE) ** -0.5, 0.25)
    batch_rows = draw_batch_rows(jax.random.fold_in(jax.random.fold_in(arg_keys[5], part), 71), part)
    return dict(factors=factors, tile_cols=tile_cols, tile_live=tile_live, coefficients=coefficients, batch_rows=batch_rows)


def reference(factors, tile_cols, tile_live, coefficients, batch_rows):
    live_mask = tile_live.astype(jnp.bfloat16)
    masked = factors * live_mask[None, :, :, None, None]
    grouped = masked.reshape(N_AUX, AUX_DEV, TILES, SLOTS, TILE, TILE)
    running = jnp.zeros((NBAS, NBAS), jnp.float32)
    for batch in range(BATCHES):
        orbital_rows = coefficients[batch_rows[batch]].reshape(OCC, TILES, TILE)
        picked = orbital_rows[:, tile_cols, :].astype(jnp.float32)

        def add_block(acc, aux_block):
            half_done = jnp.einsum('ptkxy,itky->iptx', aux_block.astype(jnp.float32), picked)
            half_done = half_done.astype(jnp.bfloat16).reshape(OCC * AUX_DEV, NBAS)
            return (acc + jnp.dot(half_done.T, half_done, preferred_element_type=jnp.float32), None)
        running, _ = lax.scan(add_block, running, grouped)
    return running * (1.0 / math.sqrt(AUX * BATCHES * OCC))
```

```python
import functools
import math

import jax
import jax.numpy as jnp
from jax import lax
from jax.experimental import pallas as pl
from jax.experimental.pallas import tpu as pltpu
from jax.sharding import PartitionSpec as P

MESH = pl.DeviceIdType.MESH
LAST = (((1,), (1,)), ((), ()))
ORDER = [sum(d * 4**s for s, d in enumerate(row)) for row in ((1, 3, 2, 0), (0, 3, 2, 1), (0, 3, 1, 2), (0, 1, 2, 3))]


def half_kernel(cols_ref, live_ref, rows_ref, coef_ref, fac_ref, out_ref, picked):
    t = pl.program_id(0)
    aux, _, slots, tile, _ = fac_ref.shape
    batches, occ = rows_ref.shape
    norb = coef_ref.shape[0]

    @pl.when(t == 0)
    def _():
        ids = lax.broadcasted_iota(jnp.int32, (norb, occ), 0)
        for b in range(batches):
            onehot = (ids == rows_ref[b : b + 1, :]).astype(jnp.float32).T.astype(jnp.bfloat16)
            picked[b * occ : (b + 1) * occ, :] = jnp.dot(
                onehot, coef_ref[...], preferred_element_type=jnp.float32
            ).astype(jnp.bfloat16)

    parts = []
    for k in range(slots):
        block = picked[:, pl.ds(pl.multiple_of(cols_ref[t, k] * tile, tile), tile)]
        parts.append(block * live_ref[t, k].astype(jnp.float32).astype(jnp.bfloat16))
    weights = jnp.concatenate(parts, axis=1)
    width = batches * occ
    for p in range(aux):
        lhs = jnp.concatenate([fac_ref[p, 0, k] for k in range(slots)], axis=1)
        out_ref[:, p * width : (p + 1) * width] = lax.dot_general(
            lhs, weights, LAST, preferred_element_type=jnp.float32
        ).astype(jnp.bfloat16)


def half_transformed(factors, tile_cols, tile_live, coefficients, batch_rows):
    aux, tiles, slots, tile, _ = factors.shape
    batches, occ = batch_rows.shape
    depth = aux * batches * occ
    smem = pl.BlockSpec(memory_space=pltpu.SMEM)
    return pl.pallas_call(
        half_kernel,
        grid=(tiles,),
        out_shape=jax.ShapeDtypeStruct((tiles * tile, depth), jnp.bfloat16),
        in_specs=[
            smem,
            smem,
            pl.BlockSpec(batch_rows.shape, lambda t: (0, 0)),
            pl.BlockSpec(coefficients.shape, lambda t: (0, 0)),
            pl.BlockSpec((aux, 1, slots, tile, tile), lambda t: (0, t, 0, 0, 0)),
        ],
        out_specs=pl.BlockSpec((tile, depth), lambda t: (t, 0)),
        scratch_shapes=[pltpu.VMEM((batches * occ, coefficients.shape[1]), jnp.bfloat16)],
        compiler_params=pltpu.CompilerParams(vmem_limit_bytes=40 * 2**20),
        cost_estimate=pl.CostEstimate(flops=2 * factors.size * batches * occ, bytes_accessed=factors.size * 2, transcendentals=0),
    )(tile_cols, tile_live, batch_rows, coefficients, factors)


def exchange_kernel(
    norm, half_ref, out_ref, h, ytx, yrx, acc, ztx, zrx, ftx, frx,
    own_sem, h_send, h_recv, y_send, y_recv, z_send, z_recv, f_send, f_recv,
):
    g, aux, b = lax.axis_index("groups"), lax.axis_index("aux"), lax.axis_index("bas")
    y, z = lax.rem(aux, 2), aux // 2
    rows = half_ref.shape[0]
    w = jnp.where(b == 0, z, 3 - z)
    packed = jnp.where(w == 0, ORDER[0], jnp.where(w == 1, ORDER[1], jnp.where(w == 2, ORDER[2], ORDER[3])))

    def dest(s):
        scale = jnp.where(s == 0, 1, jnp.where(s == 1, 4, jnp.where(s == 2, 16, 64)))
        wd = lax.rem(packed // scale, 4)
        return jnp.where(b == 0, wd, 3 - wd)

    barrier = pltpu.get_barrier_semaphore()
    for step in range(1, 16):
        other = lax.rem(aux * 2 + b + step, 16)
        pl.semaphore_signal(barrier, inc=1, device_id=(g, other // 2, lax.rem(other, 2)), device_id_type=MESH)

    mine = pl.ds(pl.multiple_of(b * rows, 1024), rows)
    own_copy = pltpu.make_async_copy(half_ref, h.at[mine], own_sem)
    own_copy.start()
    pl.semaphore_wait(barrier, 15)
    swap = pltpu.make_async_remote_copy(
        src_ref=half_ref, dst_ref=h.at[mine], send_sem=h_send, recv_sem=h_recv,
        device_id=(g, aux, 1 - b), device_id_type=MESH,
    )
    swap.start()

    def piece(o, slot):
        r = jnp.where(slot == 4, o, b * 4 + slot)
        upper = jnp.where(slot == 4, 1, jnp.where(o > r, 1, 0))
        hi, lo = jnp.maximum(o, r), jnp.minimum(o, r)
        left = h[pl.ds(pl.multiple_of(hi * 256 + upper * 128, 128), 128), :]
        right = h[pl.ds(pl.multiple_of(lo * 256, 256), 256), :]
        return lax.dot_general(left, right, LAST, preferred_element_type=jnp.float32)

    diagonal = lax.broadcasted_iota(jnp.int32, (128, 128), 0) == lax.broadcasted_iota(jnp.int32, (128, 128), 1)
    row_ids = lax.broadcasted_iota(jnp.int32, (128, 128), 0)

    def lost(block):
        rest = block - block.astype(jnp.bfloat16).astype(jnp.float32)
        return jnp.sum(jnp.where(diagonal, rest, 0.0), axis=0, keepdims=True)

    def lost_rows(first, second):
        return jnp.where(row_ids == 0, lost(first), jnp.where(row_ids == 1, lost(second), 0.0))

    CHUNKS = ((0, 256), (256, 256), (512, 128))

    def extra(zd):
        return zd // 2 == b

    def each_chunk(zd, body):
        body(0)
        body(1)

        @pl.when(extra(zd))
        def _():
            body(2)

    def y_copy(s, c):
        at, size = CHUNKS[c]
        return pltpu.make_async_remote_copy(
            src_ref=ytx.at[s, pl.ds(at, size)], dst_ref=yrx.at[s, pl.ds(at, size)],
            send_sem=y_send.at[s, c], recv_sem=y_recv.at[s, c],
            device_id=(g, z * 2 + 1 - y, b), device_id_type=MESH,
        )

    def z_copy(zd, up, c, to):
        at, size = CHUNKS[c]
        return pltpu.make_async_remote_copy(
            src_ref=ztx.at[zd, pl.ds(at, size)], dst_ref=zrx.at[up, zd, pl.ds(at, size)],
            send_sem=z_send.at[zd, c], recv_sem=z_recv.at[up, zd, c],
            device_id=(g, to * 2 + y, b), device_id_type=MESH,
        )

    own_copy.wait()

    def y_step(s, carry):
        @pl.when(s == 1)
        def _():
            swap.wait()

        zd = dest(s)
        o = zd * 2 + 1 - y

        def chunk(c):
            def one(slot, carry):
                ytx[s, pl.ds(pl.multiple_of(slot * 128, 128), 128), :] = piece(o, slot).astype(jnp.bfloat16)
                return carry

            at, size = CHUNKS[c]
            if c < 2:
                lax.fori_loop(at // 128, (at + size) // 128, one, 0)
            else:
                first, second = piece(o, lax.rem(o, 4))[:, :128], piece(o, 4)[:, 128:]
                ytx[s, 512:640, 0:128] = lost_rows(first, second).astype(jnp.bfloat16)
                ytx[s, 512:640, 128:256] = second.astype(jnp.bfloat16)
            y_copy(s, c).start()

        each_chunk(zd, chunk)
        return carry

    lax.fori_loop(0, 4, y_step, 0)

    def own_step(s, carry):
        zd = dest(s)
        o = zd * 2 + y

        def one(slot, carry):
            acc[s, pl.ds(pl.multiple_of(slot * 128, 128), 128), :] = piece(o, slot)
            return carry

        lax.fori_loop(0, jnp.where(extra(zd), 5, 4), one, 0)
        acc[s, 512:640, 0:128] = jnp.zeros((128, 128), jnp.float32)
        return carry

    lax.fori_loop(0, 4, own_step, 0)

    def add(s, c, ref):
        at, size = CHUNKS[c]
        acc[s, pl.ds(at, size), :] += ref[pl.ds(at, size), :].astype(jnp.float32)

    def chain_step(s, carry):
        zd = dest(s)
        up = jnp.where(zd > z, 0, 1)
        before = jnp.where(zd > z, z - 1, z + 1)
        has_before = jnp.logical_and(before >= 0, before < 4)

        def chunk(c):
            at, size = CHUNKS[c]
            y_copy(s, c).wait_recv()
            add(s, c, yrx.at[s])

            @pl.when(has_before)
            def _():
                z_copy(zd, up, c, before).wait_recv()
                add(s, c, zrx.at[up, zd])

            if c < 2:
                ztx[zd, pl.ds(at, size), :] = acc[s, pl.ds(at, size), :].astype(jnp.bfloat16)
            else:
                own_slot = pl.multiple_of(lax.rem(zd * 2 + y, 4) * 128, 128)
                first, second = acc[s, pl.ds(own_slot, 128), 0:128], acc[s, 512:640, 128:256]
                rest = acc[s, 512:640, 0:128] + lost_rows(first, second)
                ztx[zd, 512:640, 0:128] = rest.astype(jnp.bfloat16)
                ztx[zd, 512:640, 128:256] = second.astype(jnp.bfloat16)
            z_copy(zd, up, c, jnp.where(zd > z, z + 1, z - 1)).start()

        each_chunk(zd, chunk)
        return carry

    lax.fori_loop(0, 3, chain_step, 0)

    def f_copy(j, to, to_core, slot_at):
        return pltpu.make_async_remote_copy(
            src_ref=ftx.at[j], dst_ref=frx.at[slot_at], send_sem=f_send.at[j], recv_sem=f_recv.at[slot_at],
            device_id=(g, to, to_core), device_id_type=MESH,
        )

    def last(c):
        at, size = CHUNKS[c]
        y_copy(3, c).wait_recv()
        add(3, c, yrx.at[3])

        @pl.when(z > 0)
        def _():
            z_copy(z, 0, c, z).wait_recv()
            add(3, c, zrx.at[0, z])

        @pl.when(z < 3)
        def _():
            z_copy(z, 1, c, z).wait_recv()
            add(3, c, zrx.at[1, z])

        if c < 2:
            for j in (2 * c, 2 * c + 1):
                r = b * 4 + j

                @pl.when(r != aux)
                def _():
                    ftx[j] = acc[3, pl.ds(j * 128, 128), :].astype(jnp.bfloat16)
                    f_copy(j, r, aux // 4, lax.rem(aux, 4)).start()

    each_chunk(z, last)

    for j in range(4):
        r = b * 4 + j
        low, high = j * 256, j * 256 + 128

        @pl.when(r == aux)
        def _():
            for side in range(2):
                rest = jnp.where(diagonal, acc[3, 512 + side : 513 + side, 0:128], 0.0)
                source = acc[3, j * 128 : j * 128 + 128, 0:128] if side == 0 else acc[3, 512:640, 128:256]
                at = low + side * 128
                out_ref[at : at + 128, side * 128 : side * 128 + 128] = (source + rest) * norm
            corner = acc[3, j * 128 : j * 128 + 128, 128:256] * norm
            out_ref[low:high, 128:256] = corner
            out_ref[high : high + 128, 0:128] = corner.T

        @pl.when(r > aux)
        def _():
            out_ref[low:high, :] = acc[3, pl.ds(j * 128, 128), :] * norm

        @pl.when(r < aux)
        def _():
            out_ref[low : low + 256, 128:256] = (acc[3, pl.ds(j * 128, 128), :] * norm).T

    for j in range(4):
        r = b * 4 + j
        low, high = j * 256, j * 256 + 128

        @pl.when(r != aux)
        def _():
            f_copy(j, r, aux // 4, j).wait_recv()

        @pl.when(r > aux)
        def _():
            out_ref[high : high + 128, :] = frx[j].astype(jnp.float32) * norm

        @pl.when(r < aux)
        def _():
            out_ref[low : low + 256, 0:128] = (frx[j].astype(jnp.float32) * norm).T

    def drain(s, carry):
        zd = dest(s)
        each_chunk(zd, lambda c: y_copy(s, c).wait_send())

        @pl.when(zd != z)
        def _():
            each_chunk(zd, lambda c: z_copy(zd, 0, c, z).wait_send())

        return carry

    lax.fori_loop(0, 4, drain, 0)
    for j in range(4):
        r = b * 4 + j

        @pl.when(r != aux)
        def _():
            f_copy(j, r, aux // 4, j).wait_send()


def exchange(half, norm):
    rows, depth = half.shape
    dma = pltpu.SemaphoreType.DMA
    bf16, f32 = jnp.bfloat16, jnp.float32
    return pl.pallas_call(
        functools.partial(exchange_kernel, norm),
        out_shape=jax.ShapeDtypeStruct((rows, 256), f32),
        in_specs=[pl.BlockSpec(memory_space=pl.ANY)],
        out_specs=pl.BlockSpec(memory_space=pltpu.VMEM),
        scratch_shapes=[
            pltpu.VMEM((2 * rows, depth), bf16),
            pltpu.VMEM((4, 640, 256), bf16),
            pltpu.VMEM((4, 640, 256), bf16),
            pltpu.VMEM((4, 640, 256), f32),
            pltpu.VMEM((4, 640, 256), bf16),
            pltpu.VMEM((2, 4, 640, 256), bf16),
            pltpu.VMEM((4, 128, 256), bf16),
            pltpu.VMEM((4, 128, 256), bf16),
            dma, dma, dma, dma((4, 3)), dma((4, 3)), dma((4, 3)), dma((2, 4, 3)), dma((4,)), dma((4,)),
        ],
        compiler_params=pltpu.CompilerParams(
            collective_id=0, has_side_effects=True, vmem_limit_bytes=48 * 2**20
        ),
        cost_estimate=pl.CostEstimate(flops=2 * rows * rows * depth, bytes_accessed=half.size * 2, transcendentals=0),
    )(half)


def general(half, norm):
    everyone = lax.all_gather(half, "bas", axis=0, tiled=True)
    partial_value = lax.dot_general(half, everyone, LAST, preferred_element_type=jnp.float32)
    return lax.psum_scatter(partial_value, "aux", scatter_dimension=1, tiled=True) * norm


def on_device(factors, tile_cols, tile_live, coefficients, batch_rows):
    members = lax.axis_size("aux")
    norm = 1.0 / math.sqrt(factors.shape[0] * members * batch_rows.size)
    half = half_transformed(factors, tile_cols, tile_live, coefficients, batch_rows)
    columns = coefficients.shape[1] // members
    if members == 8 and lax.axis_size("bas") == 2 and columns == 256:
        return exchange(half, norm)
    return general(half, norm)


def solution(mesh):
    in_specs = (
        P(("groups", "aux"), "bas", None, None, None),
        P(("groups", "bas"), None),
        P(("groups", "bas"), None),
        P("groups", None),
        P("groups", None),
    )
    out_specs = P(("groups", "bas"), "aux")
    return jax.shard_map(
        on_device, mesh=mesh, in_specs=in_specs, out_specs=out_specs, check_vma=False
    )
```

```python
import functools
import math

import jax
import jax.numpy as jnp
from jax import lax
from jax.experimental import pallas as pl
from jax.experimental.pallas import tpu as pltpu
from jax.sharding import PartitionSpec as P

MESH = pl.DeviceIdType.MESH
LAST = (((1,), (1,)), ((), ()))
ORDER = [sum(d * 4**s for s, d in enumerate(row)) for row in ((1, 3, 2, 0), (0, 3, 2, 1), (0, 3, 1, 2), (0, 1, 2, 3))]


def half_kernel(cols_ref, live_ref, rows_ref, coef_ref, fac_ref, out_ref, picked):
    t = pl.program_id(0)
    aux, _, slots, tile, _ = fac_ref.shape
    batches, occ = rows_ref.shape
    norb = coef_ref.shape[0]

    @pl.when(t == 0)
    def _():
        ids = lax.broadcasted_iota(jnp.int32, (norb, occ), 0)
        for b in range(batches):
            onehot = (ids == rows_ref[b : b + 1, :]).astype(jnp.float32).T.astype(jnp.bfloat16)
            picked[b * occ : (b + 1) * occ, :] = jnp.dot(
                onehot, coef_ref[...], preferred_element_type=jnp.float32
            ).astype(jnp.bfloat16)

    parts = []
    for k in range(slots):
        block = picked[:, pl.ds(pl.multiple_of(cols_ref[k, t] * tile, tile), tile)]
        parts.append(block * live_ref[k, t].astype(jnp.float32).astype(jnp.bfloat16))
    weights = jnp.concatenate(parts, axis=1)
    width = batches * occ
    lhs = jnp.concatenate([fac_ref[:, 0, k].reshape(aux * tile, tile) for k in range(slots)], axis=1)
    half = lax.dot_general(lhs, weights, LAST, preferred_element_type=jnp.float32).astype(jnp.bfloat16)
    for p in range(aux):
        out_ref[:, p * width : (p + 1) * width] = half[p * tile : (p + 1) * tile]


def half_transformed(factors, tile_cols, tile_live, coefficients, batch_rows):
    aux, tiles, slots, tile, _ = factors.shape
    batches, occ = batch_rows.shape
    depth = aux * batches * occ
    smem = pl.BlockSpec(memory_space=pltpu.SMEM)
    return pl.pallas_call(
        half_kernel,
        grid=(tiles,),
        out_shape=jax.ShapeDtypeStruct((tiles * tile, depth), jnp.bfloat16),
        in_specs=[
            smem,
            smem,
            pl.BlockSpec(batch_rows.shape, lambda t: (0, 0)),
            pl.BlockSpec(coefficients.shape, lambda t: (0, 0)),
            pl.BlockSpec((aux, 1, slots, tile, tile), lambda t: (0, t, 0, 0, 0)),
        ],
        out_specs=pl.BlockSpec((tile, depth), lambda t: (t, 0)),
        scratch_shapes=[pltpu.VMEM((batches * occ, coefficients.shape[1]), jnp.bfloat16)],
        compiler_params=pltpu.CompilerParams(vmem_limit_bytes=40 * 2**20),
        cost_estimate=pl.CostEstimate(flops=2 * factors.size * batches * occ, bytes_accessed=factors.size * 2, transcendentals=0),
    )(tile_cols.T, tile_live.T, batch_rows, coefficients, factors)


def exchange_kernel(
    norm, half_ref, out_ref, h, tall, ytx, yrx, acc, ztx, zrx, ftx, frx,
    own_sem, h_send, h_recv, y_send, y_recv, z_send, z_recv, f_send, f_recv,
):
    g, aux, b = lax.axis_index("groups"), lax.axis_index("aux"), lax.axis_index("bas")
    y, z = lax.rem(aux, 2), aux // 2
    rows = half_ref.shape[0]
    w = jnp.where(b == 0, z, 3 - z)
    packed = jnp.where(w == 0, ORDER[0], jnp.where(w == 1, ORDER[1], jnp.where(w == 2, ORDER[2], ORDER[3])))

    def dest(s):
        scale = jnp.where(s == 0, 1, jnp.where(s == 1, 4, jnp.where(s == 2, 16, 64)))
        wd = lax.rem(packed // scale, 4)
        return jnp.where(b == 0, wd, 3 - wd)

    barrier = pltpu.get_barrier_semaphore()
    for step in range(1, 16):
        other = lax.rem(aux * 2 + b + step, 16)
        pl.semaphore_signal(barrier, inc=1, device_id=(g, other // 2, lax.rem(other, 2)), device_id_type=MESH)

    mine = pl.ds(pl.multiple_of(b * rows, 1024), rows)
    own_copy = pltpu.make_async_copy(half_ref, h.at[mine], own_sem)
    own_copy.start()
    pl.semaphore_wait(barrier, 15)
    swap = pltpu.make_async_remote_copy(
        src_ref=half_ref, dst_ref=h.at[mine], send_sem=h_send, recv_sem=h_recv,
        device_id=(g, aux, 1 - b), device_id_type=MESH,
    )
    swap.start()

    diagonal = lax.broadcasted_iota(jnp.int32, (128, 128), 0) == lax.broadcasted_iota(jnp.int32, (128, 128), 1)
    row_ids = lax.broadcasted_iota(jnp.int32, (128, 128), 0)

    def lost(block):
        rest = block - block.astype(jnp.bfloat16).astype(jnp.float32)
        return jnp.sum(jnp.where(diagonal, rest, 0.0), axis=0, keepdims=True)

    def lost_rows(first, second):
        return jnp.where(row_ids == 0, lost(first), jnp.where(row_ids == 1, lost(second), 0.0))

    CHUNKS = ((0, 256), (256, 256), (512, 128))

    def extra(zd):
        return zd // 2 == b

    def each_chunk(zd, body):
        body(0)
        body(1)

        @pl.when(extra(zd))
        def _():
            body(2)

    def y_copy(s, c):
        at, size = CHUNKS[c]
        return pltpu.make_async_remote_copy(
            src_ref=ytx.at[s, pl.ds(at, size)], dst_ref=yrx.at[s, pl.ds(at, size)],
            send_sem=y_send.at[s, c], recv_sem=y_recv.at[s, c],
            device_id=(g, z * 2 + 1 - y, b), device_id_type=MESH,
        )

    def z_copy(zd, up, c, to):
        at, size = CHUNKS[c]
        return pltpu.make_async_remote_copy(
            src_ref=ztx.at[zd, pl.ds(at, size)], dst_ref=zrx.at[up, zd, pl.ds(at, size)],
            send_sem=z_send.at[zd, c], recv_sem=z_recv.at[up, zd, c],
            device_id=(g, to * 2 + y, b), device_id_type=MESH,
        )

    own_copy.wait()

    def top(r):
        return h[pl.ds(pl.multiple_of(r * 256, 256), 128), :]

    def bottom(r):
        return h[pl.ds(pl.multiple_of(r * 256 + 128, 128), 128), :]

    def block(r):
        return h[pl.ds(pl.multiple_of(r * 256, 256), 256), :]

    def dot(left, right):
        return lax.dot_general(left, right, LAST, preferred_element_type=jnp.float32)

    def compute_step(s, carry):
        @pl.when(s == 1)
        def _():
            swap.wait()

        zd = dest(s)
        theirs, ours = zd * 2 + 1 - y, zd * 2 + y
        starts = [b * 4 + j for j in range(4)]

        def smaller(o, store):
            def one(slot, carry):
                store(pl.ds(pl.multiple_of(slot * 128, 128), 128), dot(bottom(o), block(b * 4 + slot)))
                return carry

            lax.fori_loop(0, lax.rem(o, 4), one, 0)

        def store_theirs(at, value):
            ytx[s, at, :] = value.astype(jnp.bfloat16)

        def store_ours(at, value):
            acc[s, at, :] = value

        @pl.when(extra(zd))
        def _():
            full = dot(jnp.concatenate([top(r) for r in starts] + [bottom(theirs)], axis=0), block(theirs))
            tall[...] = full
            store_theirs(pl.ds(0, 512), full[:512])
            first = tall[pl.ds(pl.multiple_of(lax.rem(theirs, 4) * 128, 128), 128), 0:128]
            second = full[512:, 128:]
            ytx[s, 512:640, 0:128] = lost_rows(first, second).astype(jnp.bfloat16)
            ytx[s, 512:640, 128:256] = second.astype(jnp.bfloat16)
            smaller(theirs, store_theirs)
            for c in range(3):
                y_copy(s, c).start()
            full = dot(jnp.concatenate([top(r) for r in starts] + [bottom(ours)], axis=0), block(ours))
            store_ours(pl.ds(0, 512), full[:512])
            acc[s, 512:640, 0:128] = jnp.zeros((128, 128), jnp.float32)
            acc[s, 512:640, 128:256] = full[512:, 128:]
            smaller(ours, store_ours)

        @pl.when(jnp.logical_and(jnp.logical_not(extra(zd)), b == 1))
        def _():
            left = jnp.concatenate([top(r) for r in starts], axis=0)
            store_theirs(pl.ds(0, 512), dot(left, block(theirs)))
            for c in range(2):
                y_copy(s, c).start()
            store_ours(pl.ds(0, 512), dot(left, block(ours)))

        @pl.when(jnp.logical_and(jnp.logical_not(extra(zd)), b == 0))
        def _():
            def one(slot, carry):
                both = dot(jnp.concatenate([bottom(theirs), bottom(ours)], axis=0), block(slot))
                at = pl.ds(pl.multiple_of(slot * 128, 128), 128)
                store_theirs(at, both[:128])
                store_ours(at, both[128:])
                return carry

            for c in range(2):
                lax.fori_loop(2 * c, 2 * c + 2, one, 0)
                y_copy(s, c).start()

        return carry

    lax.fori_loop(0, 4, compute_step, 0)

    def add(s, c, ref):
        at, size = CHUNKS[c]
        acc[s, pl.ds(at, size), :] += ref[pl.ds(at, size), :].astype(jnp.float32)

    def chain_step(s, carry):
        zd = dest(s)
        up = jnp.where(zd > z, 0, 1)
        before = jnp.where(zd > z, z - 1, z + 1)
        has_before = jnp.logical_and(before >= 0, before < 4)

        def chunk(c):
            at, size = CHUNKS[c]
            y_copy(s, c).wait_recv()
            add(s, c, yrx.at[s])

            @pl.when(has_before)
            def _():
                z_copy(zd, up, c, before).wait_recv()
                add(s, c, zrx.at[up, zd])

            if c < 2:
                ztx[zd, pl.ds(at, size), :] = acc[s, pl.ds(at, size), :].astype(jnp.bfloat16)
            else:
                own_slot = pl.multiple_of(lax.rem(zd * 2 + y, 4) * 128, 128)
                first, second = acc[s, pl.ds(own_slot, 128), 0:128], acc[s, 512:640, 128:256]
                rest = acc[s, 512:640, 0:128] + lost_rows(first, second)
                ztx[zd, 512:640, 0:128] = rest.astype(jnp.bfloat16)
                ztx[zd, 512:640, 128:256] = second.astype(jnp.bfloat16)
            z_copy(zd, up, c, jnp.where(zd > z, z + 1, z - 1)).start()

        each_chunk(zd, chunk)
        return carry

    lax.fori_loop(0, 3, chain_step, 0)

    def f_copy(j, to, to_core, slot_at):
        return pltpu.make_async_remote_copy(
            src_ref=ftx.at[j], dst_ref=frx.at[slot_at], send_sem=f_send.at[j], recv_sem=f_recv.at[slot_at],
            device_id=(g, to, to_core), device_id_type=MESH,
        )

    def last(c):
        at, size = CHUNKS[c]
        y_copy(3, c).wait_recv()
        add(3, c, yrx.at[3])

        @pl.when(z > 0)
        def _():
            z_copy(z, 0, c, z).wait_recv()
            add(3, c, zrx.at[0, z])

        @pl.when(z < 3)
        def _():
            z_copy(z, 1, c, z).wait_recv()
            add(3, c, zrx.at[1, z])

        if c < 2:
            for j in (2 * c, 2 * c + 1):
                r = b * 4 + j

                @pl.when(r != aux)
                def _():
                    ftx[j] = acc[3, pl.ds(j * 128, 128), :].astype(jnp.bfloat16)
                    f_copy(j, r, aux // 4, lax.rem(aux, 4)).start()

    each_chunk(z, last)

    for j in range(4):
        r = b * 4 + j
        low, high = j * 256, j * 256 + 128

        @pl.when(r == aux)
        def _():
            for side in range(2):
                rest = jnp.where(diagonal, acc[3, 512 + side : 513 + side, 0:128], 0.0)
                source = acc[3, j * 128 : j * 128 + 128, 0:128] if side == 0 else acc[3, 512:640, 128:256]
                at = low + side * 128
                out_ref[at : at + 128, side * 128 : side * 128 + 128] = (source + rest) * norm
            corner = acc[3, j * 128 : j * 128 + 128, 128:256] * norm
            out_ref[low:high, 128:256] = corner
            out_ref[high : high + 128, 0:128] = corner.T

        @pl.when(r > aux)
        def _():
            out_ref[low:high, :] = acc[3, pl.ds(j * 128, 128), :] * norm

        @pl.when(r < aux)
        def _():
            out_ref[low : low + 256, 128:256] = (acc[3, pl.ds(j * 128, 128), :] * norm).T

    for j in range(4):
        r = b * 4 + j
        low, high = j * 256, j * 256 + 128

        @pl.when(r != aux)
        def _():
            f_copy(j, r, aux // 4, j).wait_recv()

        @pl.when(r > aux)
        def _():
            out_ref[high : high + 128, :] = frx[j].astype(jnp.float32) * norm

        @pl.when(r < aux)
        def _():
            out_ref[low : low + 256, 0:128] = (frx[j].astype(jnp.float32) * norm).T

    def drain(s, carry):
        zd = dest(s)
        each_chunk(zd, lambda c: y_copy(s, c).wait_send())

        @pl.when(zd != z)
        def _():
            each_chunk(zd, lambda c: z_copy(zd, 0, c, z).wait_send())

        return carry

    lax.fori_loop(0, 4, drain, 0)
    for j in range(4):
        r = b * 4 + j

        @pl.when(r != aux)
        def _():
            f_copy(j, r, aux // 4, j).wait_send()


def exchange(half, norm):
    rows, depth = half.shape
    dma = pltpu.SemaphoreType.DMA
    bf16, f32 = jnp.bfloat16, jnp.float32
    return pl.pallas_call(
        functools.partial(exchange_kernel, norm),
        out_shape=jax.ShapeDtypeStruct((rows, 256), f32),
        in_specs=[pl.BlockSpec(memory_space=pl.ANY)],
        out_specs=pl.BlockSpec(memory_space=pltpu.VMEM),
        scratch_shapes=[
            pltpu.VMEM((2 * rows, depth), bf16),
            pltpu.VMEM((640, 256), f32),
            pltpu.VMEM((4, 640, 256), bf16),
            pltpu.VMEM((4, 640, 256), bf16),
            pltpu.VMEM((4, 640, 256), f32),
            pltpu.VMEM((4, 640, 256), bf16),
            pltpu.VMEM((2, 4, 640, 256), bf16),
            pltpu.VMEM((4, 128, 256), bf16),
            pltpu.VMEM((4, 128, 256), bf16),
            dma, dma, dma, dma((4, 3)), dma((4, 3)), dma((4, 3)), dma((2, 4, 3)), dma((4,)), dma((4,)),
        ],
        compiler_params=pltpu.CompilerParams(
            collective_id=0, has_side_effects=True, vmem_limit_bytes=48 * 2**20
        ),
        cost_estimate=pl.CostEstimate(flops=2 * rows * rows * depth, bytes_accessed=half.size * 2, transcendentals=0),
    )(half)


def general(half, norm):
    everyone = lax.all_gather(half, "bas", axis=0, tiled=True)
    partial_value = lax.dot_general(half, everyone, LAST, preferred_element_type=jnp.float32)
    return lax.psum_scatter(partial_value, "aux", scatter_dimension=1, tiled=True) * norm


def on_device(factors, tile_cols, tile_live, coefficients, batch_rows):
    members = lax.axis_size("aux")
    norm = 1.0 / math.sqrt(factors.shape[0] * members * batch_rows.size)
    half = half_transformed(factors, tile_cols, tile_live, coefficients, batch_rows)
    columns = coefficients.shape[1] // members
    if members == 8 and lax.axis_size("bas") == 2 and columns == 256:
        return exchange(half, norm)
    return general(half, norm)


def solution(mesh):
    in_specs = (
        P(("groups", "aux"), "bas", None, None, None),
        P(("groups", "bas"), None),
        P(("groups", "bas"), None),
        P("groups", None),
        P("groups", None),
    )
    out_specs = P(("groups", "bas"), "aux")
    return jax.shard_map(
        on_device, mesh=mesh, in_specs=in_specs, out_specs=out_specs, check_vma=False
    )
```

```python
import functools
import math

import jax
import jax.numpy as jnp
from jax import lax
from jax.experimental import pallas as pl
from jax.experimental.pallas import tpu as pltpu
from jax.sharding import PartitionSpec as P

MESH = pl.DeviceIdType.MESH
LAST = (((1,), (1,)), ((), ()))
ORDER = [sum(d * 4**s for s, d in enumerate(row)) for row in ((1, 3, 2, 0), (0, 3, 2, 1), (0, 3, 1, 2), (0, 1, 2, 3))]


def half_kernel(cols_ref, live_ref, rows_ref, coef_ref, fac_ref, out_ref, picked):
    t = pl.program_id(0)
    aux, _, slots, tile, _ = fac_ref.shape
    batches, occ = rows_ref.shape
    norb = coef_ref.shape[0]

    @pl.when(t == 0)
    def _():
        ids = lax.broadcasted_iota(jnp.int32, (norb, occ), 0)
        for b in range(batches):
            onehot = (ids == rows_ref[b : b + 1, :]).astype(jnp.float32).T.astype(jnp.bfloat16)
            picked[b * occ : (b + 1) * occ, :] = jnp.dot(
                onehot, coef_ref[...], preferred_element_type=jnp.float32
            ).astype(jnp.bfloat16)

    parts = []
    for k in range(slots):
        block = picked[:, pl.ds(pl.multiple_of(cols_ref[k, t] * tile, tile), tile)]
        parts.append(block * live_ref[k, t].astype(jnp.float32).astype(jnp.bfloat16))
    weights = jnp.concatenate(parts, axis=1)
    width = batches * occ
    lhs = jnp.concatenate([fac_ref[:, 0, k].reshape(aux * tile, tile) for k in range(slots)], axis=1)
    half = lax.dot_general(lhs, weights, LAST, preferred_element_type=jnp.float32).astype(jnp.bfloat16)
    for p in range(aux):
        out_ref[:, p * width : (p + 1) * width] = half[p * tile : (p + 1) * tile]


def half_transformed(factors, tile_cols, tile_live, coefficients, batch_rows):
    aux, tiles, slots, tile, _ = factors.shape
    batches, occ = batch_rows.shape
    depth = aux * batches * occ
    smem = pl.BlockSpec(memory_space=pltpu.SMEM)
    return pl.pallas_call(
        half_kernel,
        grid=(tiles,),
        out_shape=jax.ShapeDtypeStruct((tiles * tile, depth), jnp.bfloat16),
        in_specs=[
            smem,
            smem,
            pl.BlockSpec(batch_rows.shape, lambda t: (0, 0)),
            pl.BlockSpec(coefficients.shape, lambda t: (0, 0)),
            pl.BlockSpec((aux, 1, slots, tile, tile), lambda t: (0, t, 0, 0, 0)),
        ],
        out_specs=pl.BlockSpec((tile, depth), lambda t: (t, 0)),
        scratch_shapes=[pltpu.VMEM((batches * occ, coefficients.shape[1]), jnp.bfloat16)],
        compiler_params=pltpu.CompilerParams(vmem_limit_bytes=60 * 2**20),
        cost_estimate=pl.CostEstimate(flops=2 * factors.size * batches * occ, bytes_accessed=factors.size * 2, transcendentals=0),
    )(tile_cols.T, tile_live.T, batch_rows, coefficients, factors)


def exchange_kernel(
    norm, half_ref, out_ref, h, tall, ytx, yrx, acc, ztx, zrx, ftx, frx,
    own_sem, h_send, h_recv, y_send, y_recv, z_send, z_recv, f_send, f_recv,
):
    g, aux, b = lax.axis_index("groups"), lax.axis_index("aux"), lax.axis_index("bas")
    y, z = lax.rem(aux, 2), aux // 2
    rows = half_ref.shape[0]
    w = jnp.where(b == 0, z, 3 - z)
    packed = jnp.where(w == 0, ORDER[0], jnp.where(w == 1, ORDER[1], jnp.where(w == 2, ORDER[2], ORDER[3])))

    def dest(s):
        scale = jnp.where(s == 0, 1, jnp.where(s == 1, 4, jnp.where(s == 2, 16, 64)))
        wd = lax.rem(packed // scale, 4)
        return jnp.where(b == 0, wd, 3 - wd)

    barrier = pltpu.get_barrier_semaphore()
    for step in range(1, 16):
        other = lax.rem(aux * 2 + b + step, 16)
        pl.semaphore_signal(barrier, inc=1, device_id=(g, other // 2, lax.rem(other, 2)), device_id_type=MESH)

    mine = pl.ds(pl.multiple_of(b * rows, 1024), rows)
    own_copy = pltpu.make_async_copy(half_ref, h.at[mine], own_sem)
    own_copy.start()
    pl.semaphore_wait(barrier, 15)

    def swap(q):
        return pltpu.make_async_remote_copy(
            src_ref=half_ref.at[pl.ds(pl.multiple_of(q * 512, 512), 512)],
            dst_ref=h.at[pl.ds(pl.multiple_of(b * rows + q * 512, 512), 512)],
            send_sem=h_send.at[q], recv_sem=h_recv.at[q],
            device_id=(g, aux, 1 - b), device_id_type=MESH,
        )

    ahead = jnp.where(b == 1, jnp.where(z == 3, 0, 1), jnp.where(z == 0, 1, 0))
    swap(ahead).start()
    swap(1 - ahead).start()

    diagonal = lax.broadcasted_iota(jnp.int32, (128, 128), 0) == lax.broadcasted_iota(jnp.int32, (128, 128), 1)
    row_ids = lax.broadcasted_iota(jnp.int32, (128, 128), 0)

    def lost(block):
        rest = block - block.astype(jnp.bfloat16).astype(jnp.float32)
        return jnp.sum(jnp.where(diagonal, rest, 0.0), axis=0, keepdims=True)

    def lost_rows(first, second):
        return jnp.where(row_ids == 0, lost(first), jnp.where(row_ids == 1, lost(second), 0.0))

    CHUNKS = ((0, 256), (256, 256), (512, 128))

    def extra(zd):
        return zd // 2 == b

    def each_chunk(zd, body):
        body(0)
        body(1)

        @pl.when(extra(zd))
        def _():
            body(2)

    def y_copy(s, c):
        at, size = CHUNKS[c]
        return pltpu.make_async_remote_copy(
            src_ref=ytx.at[s, pl.ds(at, size)], dst_ref=yrx.at[s, pl.ds(at, size)],
            send_sem=y_send.at[s, c], recv_sem=y_recv.at[s, c],
            device_id=(g, z * 2 + 1 - y, b), device_id_type=MESH,
        )

    def z_copy(zd, up, c, to):
        at, size = CHUNKS[c]
        return pltpu.make_async_remote_copy(
            src_ref=ztx.at[zd, pl.ds(at, size)], dst_ref=zrx.at[up, zd, pl.ds(at, size)],
            send_sem=z_send.at[zd, c], recv_sem=z_recv.at[up, zd, c],
            device_id=(g, to * 2 + y, b), device_id_type=MESH,
        )

    own_copy.wait()

    def top(r):
        return h[pl.ds(pl.multiple_of(r * 256, 256), 128), :]

    def bottom(r):
        return h[pl.ds(pl.multiple_of(r * 256 + 128, 128), 128), :]

    def block(r):
        return h[pl.ds(pl.multiple_of(r * 256, 256), 256), :]

    def dot(left, right):
        return lax.dot_general(left, right, LAST, preferred_element_type=jnp.float32)

    def compute_step(s, carry):
        zd = dest(s)

        @pl.when(jnp.logical_not(extra(zd)))
        def _():
            swap(lax.rem(zd, 2)).wait_recv()

        theirs, ours = zd * 2 + 1 - y, zd * 2 + y
        starts = [b * 4 + j for j in range(4)]

        def smaller(o, store):
            def one(slot, carry):
                store(pl.ds(pl.multiple_of(slot * 128, 128), 128), dot(bottom(o), block(b * 4 + slot)))
                return carry

            lax.fori_loop(0, lax.rem(o, 4), one, 0)

        def store_theirs(at, value):
            ytx[s, at, :] = value.astype(jnp.bfloat16)

        def store_ours(at, value):
            acc[s, at, :] = value

        @pl.when(extra(zd))
        def _():
            full = dot(jnp.concatenate([top(r) for r in starts] + [bottom(theirs)], axis=0), block(theirs))
            tall[...] = full
            store_theirs(pl.ds(0, 512), full[:512])
            first = tall[pl.ds(pl.multiple_of(lax.rem(theirs, 4) * 128, 128), 128), 0:128]
            second = full[512:, 128:]
            ytx[s, 512:640, 0:128] = lost_rows(first, second).astype(jnp.bfloat16)
            ytx[s, 512:640, 128:256] = second.astype(jnp.bfloat16)
            smaller(theirs, store_theirs)
            for c in range(3):
                y_copy(s, c).start()
            full = dot(jnp.concatenate([top(r) for r in starts] + [bottom(ours)], axis=0), block(ours))
            store_ours(pl.ds(0, 512), full[:512])
            acc[s, 512:640, 0:128] = jnp.zeros((128, 128), jnp.float32)
            acc[s, 512:640, 128:256] = full[512:, 128:]
            smaller(ours, store_ours)

        @pl.when(jnp.logical_and(jnp.logical_not(extra(zd)), b == 1))
        def _():
            left = jnp.concatenate([top(r) for r in starts], axis=0)
            store_theirs(pl.ds(0, 512), dot(left, block(theirs)))
            for c in range(2):
                y_copy(s, c).start()
            store_ours(pl.ds(0, 512), dot(left, block(ours)))

        @pl.when(jnp.logical_and(jnp.logical_not(extra(zd)), b == 0))
        def _():
            def one(slot, carry):
                both = dot(jnp.concatenate([bottom(theirs), bottom(ours)], axis=0), block(slot))
                at = pl.ds(pl.multiple_of(slot * 128, 128), 128)
                store_theirs(at, both[:128])
                store_ours(at, both[128:])
                return carry

            for c in range(2):
                lax.fori_loop(2 * c, 2 * c + 2, one, 0)
                y_copy(s, c).start()

        return carry


    def add(s, c, ref):
        at, size = CHUNKS[c]
        acc[s, pl.ds(at, size), :] += ref[pl.ds(at, size), :].astype(jnp.float32)

    def chain_step(s, carry):
        zd = dest(s)
        up = jnp.where(zd > z, 0, 1)
        before = jnp.where(zd > z, z - 1, z + 1)
        has_before = jnp.logical_and(before >= 0, before < 4)

        def chunk(c):
            at, size = CHUNKS[c]
            y_copy(s, c).wait_recv()
            add(s, c, yrx.at[s])

            @pl.when(has_before)
            def _():
                z_copy(zd, up, c, before).wait_recv()
                add(s, c, zrx.at[up, zd])

            if c < 2:
                ztx[zd, pl.ds(at, size), :] = acc[s, pl.ds(at, size), :].astype(jnp.bfloat16)
            else:
                own_slot = pl.multiple_of(lax.rem(zd * 2 + y, 4) * 128, 128)
                first, second = acc[s, pl.ds(own_slot, 128), 0:128], acc[s, 512:640, 128:256]
                rest = acc[s, 512:640, 0:128] + lost_rows(first, second)
                ztx[zd, 512:640, 0:128] = rest.astype(jnp.bfloat16)
                ztx[zd, 512:640, 128:256] = second.astype(jnp.bfloat16)
            z_copy(zd, up, c, jnp.where(zd > z, z + 1, z - 1)).start()

        each_chunk(zd, chunk)
        return carry

    end = jnp.logical_or(z == 0, z == 3)
    lax.fori_loop(0, 2, compute_step, 0)

    @pl.when(end)
    def _():
        chain_step(0, 0)

    lax.fori_loop(2, 4, compute_step, 0)
    lax.fori_loop(jnp.where(end, 1, 0), 3, chain_step, 0)

    def f_copy(j, to, to_core, slot_at):
        return pltpu.make_async_remote_copy(
            src_ref=ftx.at[j], dst_ref=frx.at[slot_at], send_sem=f_send.at[j], recv_sem=f_recv.at[slot_at],
            device_id=(g, to, to_core), device_id_type=MESH,
        )

    def last(c):
        at, size = CHUNKS[c]
        y_copy(3, c).wait_recv()
        add(3, c, yrx.at[3])

        @pl.when(z > 0)
        def _():
            z_copy(z, 0, c, z).wait_recv()
            add(3, c, zrx.at[0, z])

        @pl.when(z < 3)
        def _():
            z_copy(z, 1, c, z).wait_recv()
            add(3, c, zrx.at[1, z])

        if c < 2:
            for j in (2 * c, 2 * c + 1):
                r = b * 4 + j

                @pl.when(r != aux)
                def _():
                    ftx[j] = acc[3, pl.ds(j * 128, 128), :].astype(jnp.bfloat16)
                    f_copy(j, r, aux // 4, lax.rem(aux, 4)).start()

    each_chunk(z, last)

    for j in range(4):
        r = b * 4 + j
        low, high = j * 256, j * 256 + 128

        @pl.when(r == aux)
        def _():
            for side in range(2):
                rest = jnp.where(diagonal, acc[3, 512 + side : 513 + side, 0:128], 0.0)
                source = acc[3, j * 128 : j * 128 + 128, 0:128] if side == 0 else acc[3, 512:640, 128:256]
                at = low + side * 128
                out_ref[at : at + 128, side * 128 : side * 128 + 128] = (source + rest) * norm
            corner = acc[3, j * 128 : j * 128 + 128, 128:256] * norm
            out_ref[low:high, 128:256] = corner
            out_ref[high : high + 128, 0:128] = corner.T

        @pl.when(r > aux)
        def _():
            out_ref[low:high, :] = acc[3, pl.ds(j * 128, 128), :] * norm

        @pl.when(r < aux)
        def _():
            out_ref[low : low + 256, 128:256] = (acc[3, pl.ds(j * 128, 128), :] * norm).T

    for j in range(4):
        r = b * 4 + j
        low, high = j * 256, j * 256 + 128

        @pl.when(r != aux)
        def _():
            f_copy(j, r, aux // 4, j).wait_recv()

        @pl.when(r > aux)
        def _():
            out_ref[high : high + 128, :] = frx[j].astype(jnp.float32) * norm

        @pl.when(r < aux)
        def _():
            out_ref[low : low + 256, 0:128] = (frx[j].astype(jnp.float32) * norm).T

    def drain(s, carry):
        zd = dest(s)
        each_chunk(zd, lambda c: y_copy(s, c).wait_send())

        @pl.when(zd != z)
        def _():
            each_chunk(zd, lambda c: z_copy(zd, 0, c, z).wait_send())

        return carry

    lax.fori_loop(0, 4, drain, 0)
    swap(0).wait_send()
    swap(1).wait_send()
    for j in range(4):
        r = b * 4 + j

        @pl.when(r != aux)
        def _():
            f_copy(j, r, aux // 4, j).wait_send()


def exchange(half, norm):
    rows, depth = half.shape
    dma = pltpu.SemaphoreType.DMA
    bf16, f32 = jnp.bfloat16, jnp.float32
    return pl.pallas_call(
        functools.partial(exchange_kernel, norm),
        out_shape=jax.ShapeDtypeStruct((rows, 256), f32),
        in_specs=[pl.BlockSpec(memory_space=pl.ANY)],
        out_specs=pl.BlockSpec(memory_space=pltpu.VMEM),
        scratch_shapes=[
            pltpu.VMEM((2 * rows, depth), bf16),
            pltpu.VMEM((640, 256), f32),
            pltpu.VMEM((4, 640, 256), bf16),
            pltpu.VMEM((4, 640, 256), bf16),
            pltpu.VMEM((4, 640, 256), f32),
            pltpu.VMEM((4, 640, 256), bf16),
            pltpu.VMEM((2, 4, 640, 256), bf16),
            pltpu.VMEM((4, 128, 256), bf16),
            pltpu.VMEM((4, 128, 256), bf16),
            dma, dma((2,)), dma((2,)), dma((4, 3)), dma((4, 3)), dma((4, 3)), dma((2, 4, 3)), dma((4,)), dma((4,)),
        ],
        compiler_params=pltpu.CompilerParams(
            collective_id=0, has_side_effects=True, vmem_limit_bytes=60 * 2**20
        ),
        cost_estimate=pl.CostEstimate(flops=2 * rows * rows * depth, bytes_accessed=half.size * 2, transcendentals=0),
    )(half)


def general(half, norm):
    everyone = lax.all_gather(half, "bas", axis=0, tiled=True)
    partial_value = lax.dot_general(half, everyone, LAST, preferred_element_type=jnp.float32)
    return lax.psum_scatter(partial_value, "aux", scatter_dimension=1, tiled=True) * norm


def on_device(factors, tile_cols, tile_live, coefficients, batch_rows):
    members = lax.axis_size("aux")
    norm = 1.0 / math.sqrt(factors.shape[0] * members * batch_rows.size)
    half = half_transformed(factors, tile_cols, tile_live, coefficients, batch_rows)
    columns = coefficients.shape[1] // members
    if members == 8 and lax.axis_size("bas") == 2 and columns == 256:
        return exchange(half, norm)
    return general(half, norm)


def solution(mesh):
    in_specs = (
        P(("groups", "aux"), "bas", None, None, None),
        P(("groups", "bas"), None),
        P(("groups", "bas"), None),
        P("groups", None),
        P("groups", None),
    )
    out_specs = P(("groups", "bas"), "aux")
    return jax.shard_map(
        on_device, mesh=mesh, in_specs=in_specs, out_specs=out_specs, check_vma=False
    )
```

```python
import functools
import math

import jax
import jax.numpy as jnp
from jax import lax
from jax.experimental import pallas as pl
from jax.experimental.pallas import tpu as pltpu
from jax.sharding import PartitionSpec as P

MESH = pl.DeviceIdType.MESH
LAST = (((1,), (1,)), ((), ()))
ORDER = [sum(d * 4**s for s, d in enumerate(row)) for row in ((1, 3, 2, 0), (0, 3, 2, 1), (0, 3, 1, 2), (0, 1, 2, 3))]


def half_kernel(cols_ref, live_ref, rows_ref, coef_ref, fac_ref, out_ref, picked):
    t = pl.program_id(0)
    aux, _, slots, tile, _ = fac_ref.shape
    batches, occ = rows_ref.shape
    norb = coef_ref.shape[0]

    @pl.when(t == 0)
    def _():
        ids = lax.broadcasted_iota(jnp.int32, (norb, occ), 0)
        for b in range(batches):
            onehot = (ids == rows_ref[b : b + 1, :]).astype(jnp.float32).T.astype(jnp.bfloat16)
            picked[b * occ : (b + 1) * occ, :] = jnp.dot(
                onehot, coef_ref[...], preferred_element_type=jnp.float32
            ).astype(jnp.bfloat16)

    parts = []
    for k in range(slots):
        block = picked[:, pl.ds(pl.multiple_of(cols_ref[k, t] * tile, tile), tile)]
        parts.append(block * live_ref[k, t].astype(jnp.float32).astype(jnp.bfloat16))
    weights = jnp.concatenate(parts, axis=1)
    width = batches * occ
    lhs = jnp.concatenate([fac_ref[:, 0, k].reshape(aux * tile, tile) for k in range(slots)], axis=1)
    half = lax.dot_general(lhs, weights, LAST, preferred_element_type=jnp.float32).astype(jnp.bfloat16)
    for p in range(aux):
        out_ref[:, p * width : (p + 1) * width] = half[p * tile : (p + 1) * tile]


def half_transformed(factors, tile_cols, tile_live, coefficients, batch_rows):
    aux, tiles, slots, tile, _ = factors.shape
    batches, occ = batch_rows.shape
    depth = aux * batches * occ
    smem = pl.BlockSpec(memory_space=pltpu.SMEM)
    return pl.pallas_call(
        half_kernel,
        grid=(tiles,),
        out_shape=jax.ShapeDtypeStruct((tiles * tile, depth), jnp.bfloat16),
        in_specs=[
            smem,
            smem,
            pl.BlockSpec(batch_rows.shape, lambda t: (0, 0)),
            pl.BlockSpec(coefficients.shape, lambda t: (0, 0)),
            pl.BlockSpec((aux, 1, slots, tile, tile), lambda t: (0, t, 0, 0, 0)),
        ],
        out_specs=pl.BlockSpec((tile, depth), lambda t: (t, 0)),
        scratch_shapes=[pltpu.VMEM((batches * occ, coefficients.shape[1]), jnp.bfloat16)],
        compiler_params=pltpu.CompilerParams(vmem_limit_bytes=60 * 2**20),
        cost_estimate=pl.CostEstimate(flops=2 * factors.size * batches * occ, bytes_accessed=factors.size * 2, transcendentals=0),
    )(tile_cols.T, tile_live.T, batch_rows, coefficients, factors)


def exchange_kernel(
    norm, half_ref, out_ref, h, tall, ytx, yrx, acc, ztx, zrx, ftx, frx,
    own_sem, h_send, h_recv, y_send, y_recv, z_send, z_recv, f_send, f_recv,
):
    g, aux, b = lax.axis_index("groups"), lax.axis_index("aux"), lax.axis_index("bas")
    y, z = lax.rem(aux, 2), aux // 2
    rows = half_ref.shape[0]
    w = jnp.where(b == 0, z, 3 - z)
    packed = jnp.where(w == 0, ORDER[0], jnp.where(w == 1, ORDER[1], jnp.where(w == 2, ORDER[2], ORDER[3])))

    def dest(s):
        scale = jnp.where(s == 0, 1, jnp.where(s == 1, 4, jnp.where(s == 2, 16, 64)))
        wd = lax.rem(packed // scale, 4)
        return jnp.where(b == 0, wd, 3 - wd)

    barrier = pltpu.get_barrier_semaphore()
    for step in range(1, 16):
        other = lax.rem(aux * 2 + b + step, 16)
        pl.semaphore_signal(barrier, inc=1, device_id=(g, other // 2, lax.rem(other, 2)), device_id_type=MESH)

    mine = pl.ds(pl.multiple_of(b * rows, 1024), rows)
    own_copy = pltpu.make_async_copy(half_ref, h.at[mine], own_sem)
    own_copy.start()
    pl.semaphore_wait(barrier, 15)

    def swap(q):
        return pltpu.make_async_remote_copy(
            src_ref=half_ref.at[pl.ds(pl.multiple_of(q * 512, 512), 512)],
            dst_ref=h.at[pl.ds(pl.multiple_of(b * rows + q * 512, 512), 512)],
            send_sem=h_send.at[q], recv_sem=h_recv.at[q],
            device_id=(g, aux, 1 - b), device_id_type=MESH,
        )

    ahead = jnp.where(b == 1, jnp.where(z == 3, 0, 1), jnp.where(z == 0, 1, 0))
    swap(ahead).start()
    swap(1 - ahead).start()

    diagonal = lax.broadcasted_iota(jnp.int32, (128, 128), 0) == lax.broadcasted_iota(jnp.int32, (128, 128), 1)
    row_ids = lax.broadcasted_iota(jnp.int32, (128, 128), 0)

    def lost(block):
        rest = block - block.astype(jnp.bfloat16).astype(jnp.float32)
        return jnp.sum(jnp.where(diagonal, rest, 0.0), axis=0, keepdims=True)

    def lost_rows(first, second):
        return jnp.where(row_ids == 0, lost(first), jnp.where(row_ids == 1, lost(second), 0.0))

    CHUNKS = ((0, 256), (256, 256), (512, 128))

    def extra(zd):
        return zd // 2 == b

    def each_chunk(zd, body):
        body(0)
        body(1)

        @pl.when(extra(zd))
        def _():
            body(2)

    def y_copy(s, c):
        at, size = CHUNKS[c]
        return pltpu.make_async_remote_copy(
            src_ref=ytx.at[s, pl.ds(at, size)], dst_ref=yrx.at[s, pl.ds(at, size)],
            send_sem=y_send.at[s, c], recv_sem=y_recv.at[s, c],
            device_id=(g, z * 2 + 1 - y, b), device_id_type=MESH,
        )

    def z_copy(zd, up, c, to):
        at, size = CHUNKS[c]
        return pltpu.make_async_remote_copy(
            src_ref=ztx.at[zd, pl.ds(at, size)], dst_ref=zrx.at[up, zd, pl.ds(at, size)],
            send_sem=z_send.at[zd, c], recv_sem=z_recv.at[up, zd, c],
            device_id=(g, to * 2 + y, b), device_id_type=MESH,
        )

    own_copy.wait()

    def top(r):
        return h[pl.ds(pl.multiple_of(r * 256, 256), 128), :]

    def bottom(r):
        return h[pl.ds(pl.multiple_of(r * 256 + 128, 128), 128), :]

    def block(r):
        return h[pl.ds(pl.multiple_of(r * 256, 256), 256), :]

    def dot(left, right):
        return lax.dot_general(left, right, LAST, preferred_element_type=jnp.float32)

    def compute_step(s, carry):
        zd = dest(s)

        @pl.when(jnp.logical_not(extra(zd)))
        def _():
            swap(lax.rem(zd, 2)).wait_recv()

        theirs, ours = zd * 2 + 1 - y, zd * 2 + y
        starts = [b * 4 + j for j in range(4)]

        def smaller(o, store):
            def one(slot, carry):
                store(pl.ds(pl.multiple_of(slot * 128, 128), 128), dot(bottom(o), block(b * 4 + slot)))
                return carry

            lax.fori_loop(0, lax.rem(o, 4), one, 0)

        def store_theirs(at, value):
            ytx[s, at, :] = value.astype(jnp.bfloat16)

        def store_ours(at, value):
            acc[s, at, :] = value

        @pl.when(extra(zd))
        def _():
            full = dot(jnp.concatenate([top(r) for r in starts] + [bottom(theirs)], axis=0), block(theirs))
            tall[...] = full
            store_theirs(pl.ds(0, 512), full[:512])
            first = tall[pl.ds(pl.multiple_of(lax.rem(theirs, 4) * 128, 128), 128), 0:128]
            second = full[512:, 128:]
            ytx[s, 512:640, 0:128] = lost_rows(first, second).astype(jnp.bfloat16)
            ytx[s, 512:640, 128:256] = second.astype(jnp.bfloat16)
            smaller(theirs, store_theirs)
            for c in range(3):
                y_copy(s, c).start()
            full = dot(jnp.concatenate([top(r) for r in starts] + [bottom(ours)], axis=0), block(ours))
            store_ours(pl.ds(0, 512), full[:512])
            acc[s, 512:640, 0:128] = jnp.zeros((128, 128), jnp.float32)
            acc[s, 512:640, 128:256] = full[512:, 128:]
            smaller(ours, store_ours)

        @pl.when(jnp.logical_and(jnp.logical_not(extra(zd)), b == 1))
        def _():
            left = jnp.concatenate([top(r) for r in starts], axis=0)
            store_theirs(pl.ds(0, 512), dot(left, block(theirs)))
            for c in range(2):
                y_copy(s, c).start()
            store_ours(pl.ds(0, 512), dot(left, block(ours)))

        @pl.when(jnp.logical_and(jnp.logical_not(extra(zd)), b == 0))
        def _():
            def one(slot, carry):
                both = dot(jnp.concatenate([bottom(theirs), bottom(ours)], axis=0), block(slot))
                at = pl.ds(pl.multiple_of(slot * 128, 128), 128)
                store_theirs(at, both[:128])
                store_ours(at, both[128:])
                return carry

            for c in range(2):
                lax.fori_loop(2 * c, 2 * c + 2, one, 0)
                y_copy(s, c).start()

        return carry


    def add(s, c, ref):
        at, size = CHUNKS[c]
        acc[s, pl.ds(at, size), :] += ref[pl.ds(at, size), :].astype(jnp.float32)

    def chain_step(s, carry):
        zd = dest(s)
        up = jnp.where(zd > z, 0, 1)
        before = jnp.where(zd > z, z - 1, z + 1)
        has_before = jnp.logical_and(before >= 0, before < 4)

        def chunk(c):
            at, size = CHUNKS[c]
            y_copy(s, c).wait_recv()
            add(s, c, yrx.at[s])

            @pl.when(has_before)
            def _():
                z_copy(zd, up, c, before).wait_recv()
                add(s, c, zrx.at[up, zd])

            if c < 2:
                ztx[zd, pl.ds(at, size), :] = acc[s, pl.ds(at, size), :].astype(jnp.bfloat16)
            else:
                own_slot = pl.multiple_of(lax.rem(zd * 2 + y, 4) * 128, 128)
                first, second = acc[s, pl.ds(own_slot, 128), 0:128], acc[s, 512:640, 128:256]
                rest = acc[s, 512:640, 0:128] + lost_rows(first, second)
                ztx[zd, 512:640, 0:128] = rest.astype(jnp.bfloat16)
                ztx[zd, 512:640, 128:256] = second.astype(jnp.bfloat16)
            z_copy(zd, up, c, jnp.where(zd > z, z + 1, z - 1)).start()

        each_chunk(zd, chunk)
        return carry

    end = jnp.logical_or(z == 0, z == 3)
    lax.fori_loop(0, 2, compute_step, 0)

    @pl.when(end)
    def _():
        chain_step(0, 0)

    lax.fori_loop(2, 4, compute_step, 0)
    lax.fori_loop(jnp.where(end, 1, 0), 3, chain_step, 0)

    def f_copy(j, to, to_core, slot_at):
        return pltpu.make_async_remote_copy(
            src_ref=ftx.at[j], dst_ref=frx.at[slot_at], send_sem=f_send.at[j], recv_sem=f_recv.at[slot_at],
            device_id=(g, to, to_core), device_id_type=MESH,
        )

    def last(c):
        at, size = CHUNKS[c]
        y_copy(3, c).wait_recv()
        add(3, c, yrx.at[3])

        @pl.when(z > 0)
        def _():
            z_copy(z, 0, c, z).wait_recv()
            add(3, c, zrx.at[0, z])

        @pl.when(z < 3)
        def _():
            z_copy(z, 1, c, z).wait_recv()
            add(3, c, zrx.at[1, z])

        if c < 2:
            for j in (2 * c, 2 * c + 1):
                r = b * 4 + j

                @pl.when(r != aux)
                def _():
                    ftx[j] = acc[3, pl.ds(j * 128, 128), :].astype(jnp.bfloat16)
                    f_copy(j, r, aux // 4, lax.rem(aux, 4)).start()

    each_chunk(z, last)

    for j in range(4):
        r = b * 4 + j
        low, high = j * 256, j * 256 + 128

        @pl.when(r == aux)
        def _():
            for side in range(2):
                rest = jnp.where(diagonal, acc[3, 512 + side : 513 + side, 0:128], 0.0)
                source = acc[3, j * 128 : j * 128 + 128, 0:128] if side == 0 else acc[3, 512:640, 128:256]
                at = low + side * 128
                out_ref[at : at + 128, side * 128 : side * 128 + 128] = (source + rest) * norm
            corner = acc[3, j * 128 : j * 128 + 128, 128:256] * norm
            out_ref[low:high, 128:256] = corner
            out_ref[high : high + 128, 0:128] = corner.T

        @pl.when(r > aux)
        def _():
            out_ref[low:high, :] = acc[3, pl.ds(j * 128, 128), :] * norm

        @pl.when(r < aux)
        def _():
            out_ref[low : low + 256, 128:256] = (acc[3, pl.ds(j * 128, 128), :] * norm).T

    for j in range(4):
        r = b * 4 + j
        low, high = j * 256, j * 256 + 128

        @pl.when(r != aux)
        def _():
            f_copy(j, r, aux // 4, j).wait_recv()

        @pl.when(r > aux)
        def _():
            out_ref[high : high + 128, :] = frx[j].astype(jnp.float32) * norm

        @pl.when(r < aux)
        def _():
            out_ref[low : low + 256, 0:128] = (frx[j].astype(jnp.float32) * norm).T

    def drain(s, carry):
        zd = dest(s)
        each_chunk(zd, lambda c: y_copy(s, c).wait_send())

        @pl.when(zd != z)
        def _():
            each_chunk(zd, lambda c: z_copy(zd, 0, c, z).wait_send())

        return carry

    lax.fori_loop(0, 4, drain, 0)
    swap(0).wait_send()
    swap(1).wait_send()
    for j in range(4):
        r = b * 4 + j

        @pl.when(r != aux)
        def _():
            f_copy(j, r, aux // 4, j).wait_send()


def exchange(half, norm):
    rows, depth = half.shape
    dma = pltpu.SemaphoreType.DMA
    bf16, f32 = jnp.bfloat16, jnp.float32
    return pl.pallas_call(
        functools.partial(exchange_kernel, norm),
        out_shape=jax.ShapeDtypeStruct((rows, 256), f32),
        in_specs=[pl.BlockSpec(memory_space=pl.ANY)],
        out_specs=pl.BlockSpec(memory_space=pltpu.VMEM),
        scratch_shapes=[
            pltpu.VMEM((2 * rows, depth), bf16),
            pltpu.VMEM((640, 256), f32),
            pltpu.VMEM((4, 640, 256), bf16),
            pltpu.VMEM((4, 640, 256), bf16),
            pltpu.VMEM((4, 640, 256), f32),
            pltpu.VMEM((4, 640, 256), bf16),
            pltpu.VMEM((2, 4, 640, 256), bf16),
            pltpu.VMEM((4, 128, 256), bf16),
            pltpu.VMEM((4, 128, 256), bf16),
            dma, dma((2,)), dma((2,)), dma((4, 3)), dma((4, 3)), dma((4, 3)), dma((2, 4, 3)), dma((4,)), dma((4,)),
        ],
        compiler_params=pltpu.CompilerParams(
            collective_id=0, has_side_effects=True, vmem_limit_bytes=52 * 2**20
        ),
        cost_estimate=pl.CostEstimate(flops=2 * rows * rows * depth, bytes_accessed=half.size * 2, transcendentals=0),
    )(half)


def general(half, norm):
    everyone = lax.all_gather(half, "bas", axis=0, tiled=True)
    partial_value = lax.dot_general(half, everyone, LAST, preferred_element_type=jnp.float32)
    return lax.psum_scatter(partial_value, "aux", scatter_dimension=1, tiled=True) * norm


def on_device(factors, tile_cols, tile_live, coefficients, batch_rows):
    members = lax.axis_size("aux")
    norm = 1.0 / math.sqrt(factors.shape[0] * members * batch_rows.size)
    half = half_transformed(factors, tile_cols, tile_live, coefficients, batch_rows)
    columns = coefficients.shape[1] // members
    if members == 8 and lax.axis_size("bas") == 2 and columns == 256:
        return exchange(half, norm)
    return general(half, norm)


def solution(mesh):
    in_specs = (
        P(("groups", "aux"), "bas", None, None, None),
        P(("groups", "bas"), None),
        P(("groups", "bas"), None),
        P("groups", None),
        P("groups", None),
    )
    out_specs = P(("groups", "bas"), "aux")
    return jax.shard_map(
        on_device, mesh=mesh, in_specs=in_specs, out_specs=out_specs, check_vma=False
    )
```
